512 devices in a mesh: table: 128 (over z, y, core), mp: 4 (over x).
Axes of the slice: x: 4, y: 8, z: 8, core: 2. Of those that a mesh axis runs over, the one named last changes fastest.
Arguments:
- replay: bfloat16 [65536, 1024], P('table'), may hold values from -8 to 8
- request_rows: int32 [128, 128, 1], P('table'), may hold values from 0 to 506
- request_count: int32 [128, 128], P('table'), may hold values from 0 to 1
- actions: int32 [5, 16384], P(None, 'table'), may hold values from 0 to 255, as said below
- rewards: float32 [5, 16384], P(None, 'table'), may hold values from -4 to 4
- w_in: bfloat16 [1024, 2048], P('table', 'mp'), may hold values from -0.75 to 0.75
- w_out: bfloat16 [1024, 2048], P('table', 'mp'), may hold values from -1 to 1
- w_pol: bfloat16 [1024, 256], replicated, may hold values from -4 to 4
- w_val: bfloat16 [1024], replicated, may hold values from -0.1875 to 0.1875
- embed: bfloat16 [256, 1024], replicated, may hold values from -6 to 6
- gain: float32 [1024], replicated, may hold values from 0.5 to 1.5
Outputs:
- grad_pol: float32 [1024, 256], P('table')
- grad_embed: float32 [256, 1024], P('table')
- grad_val: float32 [1024], P('table')
The draws below stay inside these ranges and needn't reach their ends.
Inputs may be any that keep to these rules, and one draw needn't show every extreme that they name: `request_rows`: each names the first of 6 consecutive rows of the owner's shard. `request_count`: slots below the count are used, the others are padding. The law of an unroll's actions depends on its requester and its owner.
All inputs are finite; a program needn't handle non-finite values.
Results may differ from the reference program's by a relative error of at most 0.025.
Values may be sent and summed in bfloat16 or wider, within the bound.
No kernel may reach another device: no remote copies, remote signals or barrier semaphores. Data moves between devices by JAX's collectives and lax.ppermute only.
A program may use at most 64 MiB of HBM per device.

```python
import jax
import jax.numpy as jnp
from jax import lax

D = 1024
FF = 2048
ACTIONS = 256
STEPS = 5
CAP = 1
ROWS_DEV = 512
ROWS = 65536
UNROLLS = 16384
N_TABLE = 128
N_MP = 4


def draw_replay(key, part):
    key = jax.random.fold_in(key, 1)
    values_raw = jnp.clip(jax.random.normal(key, (ROWS, D), jnp.float32), -6.0, 6.0)
    return values_raw.astype(jnp.bfloat16)


def draw_w_pol(key, part):
    key = jax.random.fold_in(key, 2)
    values_raw = jnp.clip(jax.random.normal(key, (D, ACTIONS), jnp.float32), -6.0, 6.0) * D ** (-0.5)
    return values_raw.astype(jnp.bfloat16)


def draw_actions(key, part):
    key = jax.random.fold_in(key, 3)
    block_width = ACTIONS // N_TABLE
    unroll_ids = jnp.arange(UNROLLS, dtype=jnp.int32)
    requester = unroll_ids // (N_TABLE * CAP)
    owner = unroll_ids // CAP % N_TABLE
    kinds = jax.random.randint(jax.random.fold_in(key, 1), (STEPS, UNROLLS), 0, 5)
    inside = jax.random.randint(jax.random.fold_in(key, 2), (STEPS, UNROLLS), 0, block_width)
    anywhere = jax.random.randint(jax.random.fold_in(key, 4), (STEPS, UNROLLS), 0, ACTIONS)
    block_pair = (owner - requester) % N_TABLE
    block_own = requester
    block_before = (requester + N_TABLE - 1) % N_TABLE
    block_far = (requester + N_TABLE // 2) % N_TABLE
    chosen_block = jnp.where(kinds == 0, block_pair[None, :], jnp.where(kinds == 1, block_own[None, :], jnp.where(kinds == 2, block_before[None, :], block_far[None, :])))
    biased = chosen_block * block_width + inside
    return jnp.where(kinds == 4, anywhere, biased).astype(jnp.int32)


def plant(values, rng, least, largest):
    extent = values.shape
    spot = [jax.random.randint(jax.random.fold_in(rng, axis), (), 0, extent[axis]) for axis in range(len(extent))]
    values = values.at[tuple(spot)].set(least)
    longest = extent.index(max(extent))
    spot[longest] = (spot[longest] + 1) % extent[longest]
    return values.at[tuple(spot)].set(largest)


def strengthened(result, rng, source, target, blocks, factor):
    owner, partner = [(jnp.arange(result.shape[axis_at]) // (result.shape[axis_at] // blocks)).reshape([-1 if axis == axis_at else 1 for axis in range(result.ndim)]) for axis_at in (source, target)]
    chosen = jax.random.permutation(rng, blocks)[partner]
    strong = (owner == chosen) | (owner == (partner + blocks // 2) % blocks)
    return jnp.where(strong, factor * result, result)


def levels(stream_key, extent, cuts, least, top_value):
    def one(axis_at, blocks):
        steps = jax.random.uniform(jax.random.fold_in(jax.random.fold_in(stream_key, 6), axis_at), (blocks,), jnp.float32, least / len(cuts), top_value / len(cuts))
        return jnp.repeat(jnp.exp(steps), extent[axis_at] // blocks).reshape((-1,) + (1,) * (len(extent) - axis_at - 1))

    factor_of = one(*cuts[0])
    for cut in cuts[1:]:
        factor_of = factor_of * one(*cut)
    return factor_of


def scatter_about(rng, dims, scale, most, shards=(), kind=jnp.bfloat16):
    values = scale * jax.random.normal(rng, dims, jnp.float32)
    if shards:
        values = values * levels(rng, dims, shards, -0.22, 0.18)
    return jnp.clip(values, -most, most).astype(kind)


def heavy_noise(stream_key, dims, deviation, limit, shards, heavy, held_as=jnp.bfloat16):
    entries = deviation * jax.random.normal(stream_key, dims, jnp.float32)
    if shards:
        entries = entries * levels(stream_key, dims, shards, -0.22, 0.18)
    return jnp.clip(strengthened(entries, jax.random.fold_in(stream_key, 3), *heavy), -limit, limit).astype(held_as)


def setup_inputs(seed: int = 0) -> dict:
    streams_of = jax.random.split(jax.random.key(seed), 12)
    return {
        "replay": draw_replay(jax.random.fold_in(streams_of[11], 71), 0),
        "request_rows": plant(jax.random.randint(streams_of[1], (N_TABLE, N_TABLE, CAP), 0, ROWS_DEV - STEPS), jax.random.fold_in(streams_of[1], 1), 0, (ROWS_DEV - STEPS) - 1).astype(jnp.int32),
        "request_count": plant(jax.random.randint(streams_of[2], (N_TABLE, N_TABLE), 0, CAP + 1), jax.random.fold_in(streams_of[2], 1), 0, CAP).astype(jnp.int32),
        "actions": draw_actions(jax.random.fold_in(streams_of[11], 71), 0),
        "rewards": scatter_about(streams_of[4], (STEPS, UNROLLS), 1.0, 4.0, ((1, 128),), jnp.float32),
        "w_in": heavy_noise(streams_of[5], (D, FF), D ** -0.5, 0.75, ((0, 128), (1, 4)), (0, 1, 128, 5.5)),
        "w_out": heavy_noise(streams_of[6], (D, FF), (FF // 4) ** -0.5, 1.0, ((0, 128), (1, 4)), (0, 1, 128, 5.5)),
        "w_pol": draw_w_pol(jax.random.fold_in(streams_of[11], 71), 0),
        "w_val": scatter_about(streams_of[8], (D,), D ** -0.5, 0.1875),
        "embed": scatter_about(streams_of[9], (ACTIONS, D), 1.0, 6.0),
        "gain": jnp.clip(1.0 + 0.1 * jax.random.normal(streams_of[10], (D,), jnp.float32), 0.5, 1.5),
    }


discount = 0.997
epsilon = 1e-06

def normalize(vector, gain):
    factor = lax.rsqrt(lax.optimization_barrier(jnp.mean(vector * vector, axis=-1, keepdims=True)) + epsilon)
    return vector * factor * gain

def norm_back(vector, upstream, gain):
    factor = lax.rsqrt(lax.optimization_barrier(jnp.mean(vector * vector, axis=-1, keepdims=True)) + epsilon)
    unit_vec = vector * factor
    scaled = upstream * gain
    return factor * (scaled - unit_vec * lax.optimization_barrier(jnp.mean(scaled * unit_vec, axis=-1, keepdims=True)))

def split_product(left, weight):
    block_cols = weight.shape[1] // N_MP
    summed = jnp.zeros((left.shape[0], weight.shape[0]), jnp.float32)
    for member in range(N_MP):
        partial_term = lax.dot_general(left[:, member * block_cols:(member + 1) * block_cols], weight[:, member * block_cols:(member + 1) * block_cols], (((1,), (1,)), ((), ())), preferred_element_type=jnp.float32)
        rounded = lax.optimization_barrier(partial_term.astype(jnp.bfloat16))
        summed = summed + rounded.astype(jnp.float32)
    return summed

def reference(replay, request_rows, request_count, actions, rewards, w_in, w_out, w_pol, w_val, embed, gain):
    group_size = N_TABLE * CAP
    owners = jnp.arange(N_TABLE, dtype=jnp.int32)
    firsts = request_rows + (owners * ROWS_DEV)[:, None, None]
    firsts = jnp.transpose(firsts, (1, 0, 2)).reshape(UNROLLS)
    slots = jnp.arange(CAP, dtype=jnp.int32)
    used = (slots[None, None, :] < request_count[:, :, None]).astype(jnp.float32)
    used = jnp.transpose(used, (1, 0, 2)).reshape(UNROLLS)
    offsets = jnp.arange(STEPS + 1, dtype=jnp.int32)
    action_ids = jnp.arange(ACTIONS, dtype=jnp.int32)

    def group_terms(totals, group_id):
        offset = (group_id * group_size).astype(jnp.int32)
        first_rows = lax.dynamic_slice_in_dim(firsts, offset, group_size)
        used_rows = lax.dynamic_slice_in_dim(used, offset, group_size)
        moves = lax.dynamic_slice_in_dim(actions, offset, group_size, 1)
        payoff = lax.dynamic_slice_in_dim(rewards, offset, group_size, 1)
        observed = jnp.take(replay, first_rows[None, :] + offsets[:, None], axis=0)
        flat_obs = observed.reshape((STEPS + 1) * group_size, D).astype(jnp.float32)
        target_in = normalize(flat_obs, gain).astype(jnp.bfloat16)
        target_logits = jnp.dot(target_in, w_pol, preferred_element_type=jnp.float32)
        target_values = jnp.dot(target_in, w_val, preferred_element_type=jnp.float32).reshape(STEPS + 1, group_size)
        policy_targets = jax.nn.softmax(target_logits, axis=-1)
        value_targets = jnp.concatenate([payoff + discount * target_values[1:], target_values[STEPS:]], axis=0)
        latent = observed[0].astype(jnp.float32)
        latents = [latent]
        mixeds = []
        preacts = []
        onehots = []
        for position in range(STEPS):
            onehot = (moves[position][:, None] == action_ids[None, :]).astype(jnp.bfloat16)
            mixed = latent + jnp.dot(onehot, embed, preferred_element_type=jnp.float32)
            normed = normalize(mixed, gain).astype(jnp.bfloat16)
            preact = jnp.dot(normed, w_in, preferred_element_type=jnp.float32)
            hidden = jax.nn.silu(preact).astype(jnp.bfloat16)
            latent = mixed + split_product(hidden, w_out)
            latents.append(latent)
            mixeds.append(mixed)
            preacts.append(preact)
            onehots.append(onehot)
        stacked = jnp.stack(latents).reshape((STEPS + 1) * group_size, D)
        head_in = normalize(stacked, gain).astype(jnp.bfloat16)
        logits = jnp.dot(head_in, w_pol, preferred_element_type=jnp.float32)
        values = jnp.dot(head_in, w_val, preferred_element_type=jnp.float32)
        row_weight = jnp.tile(used_rows / (N_TABLE * CAP), STEPS + 1)
        logit_grad = (row_weight[:, None] * (jax.nn.softmax(logits, axis=-1) - policy_targets)).astype(jnp.bfloat16)
        value_grad = 2.0 * row_weight * (values - value_targets.reshape(-1))
        grad_pol = lax.dot_general(head_in, logit_grad, (((0,), (0,)), ((), ())), preferred_element_type=jnp.float32)
        grad_val = lax.optimization_barrier(jnp.sum(head_in.astype(jnp.float32) * value_grad[:, None], axis=0))
        head_grad = jnp.dot(logit_grad, w_pol.T, preferred_element_type=jnp.float32) + value_grad[:, None] * w_val.astype(jnp.float32)[None, :]
        head_back = norm_back(stacked, head_grad, gain).reshape(STEPS + 1, group_size, D)
        cotangent = head_back[STEPS]
        grad_embed = jnp.zeros((ACTIONS, D), jnp.float32)
        for position in reversed(range(STEPS)):
            hidden_grad = jnp.dot(cotangent.astype(jnp.bfloat16), w_out, preferred_element_type=jnp.float32)
            sigmoid_val = jax.nn.sigmoid(preacts[position])
            preact_grad = (hidden_grad * sigmoid_val * (1.0 + preacts[position] * (1.0 - sigmoid_val))).astype(jnp.bfloat16)
            normed_grad = split_product(preact_grad, w_in)
            mixed_grad = cotangent + norm_back(mixeds[position], normed_grad, gain)
            grad_embed = grad_embed + lax.dot_general(onehots[position], mixed_grad.astype(jnp.bfloat16), (((0,), (0,)), ((), ())), preferred_element_type=jnp.float32)
            cotangent = mixed_grad + head_back[position]
        return ((totals[0] + grad_pol, totals[1] + grad_embed, totals[2] + grad_val), None)
    start_totals = (jnp.zeros((D, ACTIONS), jnp.float32), jnp.zeros((ACTIONS, D), jnp.float32), jnp.zeros((D,), jnp.float32))
    results, unused_out = lax.scan(group_terms, start_totals, jnp.arange(N_TABLE, dtype=jnp.int32))
    return (results[0], results[1], results[2])
```

```python
import jax
import jax.numpy as jnp
from jax import lax
from jax.sharding import PartitionSpec as P

discount = 0.997
epsilon = 1e-06


def normalize(vector, gain):
    factor = lax.rsqrt(jnp.mean(vector * vector, axis=-1, keepdims=True) + epsilon)
    return vector * factor * gain


def norm_back(vector, upstream, gain):
    factor = lax.rsqrt(jnp.mean(vector * vector, axis=-1, keepdims=True) + epsilon)
    unit_vec = vector * factor
    scaled = upstream * gain
    return factor * (scaled - unit_vec * jnp.mean(scaled * unit_vec, axis=-1, keepdims=True))


def cols_product(left, weight):
    return lax.dot_general(
        left, weight, (((1,), (1,)), ((), ())), preferred_element_type=jnp.float32
    )


def rows_product(left, right):
    return lax.dot_general(
        left, right, (((0,), (0,)), ((), ())), preferred_element_type=jnp.float32
    )


def fetch_unrolls(replay, request_rows, request_count, steps, tables, members):
    member = lax.axis_index("mp")
    share = tables // members
    width = replay.shape[1]
    firsts = request_rows[0, :, 0].reshape(share, members)
    firsts = lax.dynamic_index_in_dim(firsts, member, 1, keepdims=False)
    counts = lax.dynamic_index_in_dim(
        request_count[0].reshape(share, members), member, 1, keepdims=False
    )
    used = (counts > 0).astype(jnp.float32)
    offsets = jnp.arange(8, dtype=jnp.int32)
    positions = firsts[:, None] + offsets[None, :]
    row_ids = jnp.arange(replay.shape[0], dtype=jnp.int32)
    picks = (positions.reshape(-1)[:, None] == row_ids[None, :]).astype(jnp.bfloat16)
    rows = jnp.dot(picks, replay, preferred_element_type=jnp.float32).reshape(share, 8, width)
    rows = jnp.where(offsets[None, :, None] <= steps, rows, used[:, None, None])
    rows = rows.astype(jnp.bfloat16)
    swap = [
        ((members * a + b) * members + d, (members * a + d) * members + b)
        for a in range(share)
        for b in range(members)
        for d in range(members)
    ]
    rows = lax.ppermute(rows, ("table", "mp"), swap)
    groups = [[members * a + d for a in range(share)] for d in range(members)]
    rows = lax.all_to_all(
        rows, "table", split_axis=0, concat_axis=0, tiled=True, axis_index_groups=groups
    )
    observed = rows[:, : steps + 1].transpose(1, 0, 2)
    return observed, rows[:, steps + 1, 0].astype(jnp.float32)


def gather_weights(w_in, w_out, tables, members):
    both = jnp.concatenate([w_in, w_out], axis=0)
    full = lax.all_gather(both, ("table", "mp"), axis=0, tiled=True)
    rows, cols = w_in.shape
    full = full.reshape(tables, members, 2, rows, cols).transpose(2, 0, 3, 1, 4)
    full = full.reshape(2, tables * rows, members * cols)
    return full[0], full[1]


def sum_over_tables(partial, tables):
    sent = partial.astype(jnp.bfloat16)
    parts = lax.all_to_all(sent, "table", split_axis=0, concat_axis=0, tiled=True)
    return jnp.sum(parts.astype(jnp.float32), axis=0)


def per_device(
    replay, request_rows, request_count, actions, rewards, w_in, w_out, w_pol, w_val, embed, gain
):
    tables = lax.axis_size("table")
    members = lax.axis_size("mp")
    member = lax.axis_index("mp")
    share = tables // members
    features = replay.shape[1]
    steps = actions.shape[0]
    num_actions = w_pol.shape[1]
    full_in, full_out = gather_weights(w_in, w_out, tables, members)
    observed, used_rows = fetch_unrolls(
        replay, request_rows, request_count, steps, tables, members
    )
    actions = lax.dynamic_index_in_dim(
        actions.reshape(steps, share, members), member, 2, keepdims=False
    )
    rewards = lax.dynamic_index_in_dim(
        rewards.reshape(steps, share, members), member, 2, keepdims=False
    )
    flat_obs = observed.reshape((steps + 1) * share, features).astype(jnp.float32)
    target_in = normalize(flat_obs, gain).astype(jnp.bfloat16)
    target_logits = jnp.dot(target_in, w_pol, preferred_element_type=jnp.float32)
    target_values = jnp.dot(target_in, w_val, preferred_element_type=jnp.float32).reshape(
        steps + 1, share
    )
    policy_targets = jax.nn.softmax(target_logits, axis=-1)
    value_targets = jnp.concatenate(
        [rewards + discount * target_values[1:], target_values[steps:]], axis=0
    )
    action_ids = jnp.arange(num_actions, dtype=jnp.int32)
    latent = observed[0].astype(jnp.float32)
    latents = [latent]
    mixeds = []
    preacts = []
    onehots = []
    for position in range(steps):
        onehot = (actions[position][:, None] == action_ids[None, :]).astype(jnp.bfloat16)
        mixed = latent + jnp.dot(onehot, embed, preferred_element_type=jnp.float32)
        normed = normalize(mixed, gain).astype(jnp.bfloat16)
        preact = jnp.dot(normed, full_in, preferred_element_type=jnp.float32)
        hidden = jax.nn.silu(preact).astype(jnp.bfloat16)
        latent = mixed + cols_product(hidden, full_out)
        latents.append(latent)
        mixeds.append(mixed)
        preacts.append(preact)
        onehots.append(onehot)
    stacked = jnp.stack(latents).reshape((steps + 1) * share, features)
    head_in = normalize(stacked, gain).astype(jnp.bfloat16)
    logits = jnp.dot(head_in, w_pol, preferred_element_type=jnp.float32)
    values = jnp.dot(head_in, w_val, preferred_element_type=jnp.float32)
    row_weight = jnp.tile(used_rows / tables, steps + 1)
    logit_grad = (row_weight[:, None] * (jax.nn.softmax(logits, axis=-1) - policy_targets)).astype(
        jnp.bfloat16
    )
    value_grad = 2.0 * row_weight * (values - value_targets.reshape(-1))
    grad_pol = rows_product(head_in, logit_grad)
    grad_val = jnp.sum(head_in.astype(jnp.float32) * value_grad[:, None], axis=0)
    head_grad = (
        cols_product(logit_grad, w_pol)
        + value_grad[:, None] * w_val.astype(jnp.float32)[None, :]
    )
    rows_pol = features // tables
    lane = jnp.arange(128, dtype=jnp.int32)
    val_block = jnp.where(lane == 0, grad_val.reshape(tables, rows_pol, 1), 0.0)
    pol_val = jnp.concatenate([grad_pol.reshape(tables, rows_pol, num_actions), val_block], axis=2)
    pol_val = sum_over_tables(pol_val, tables)
    head_back = norm_back(stacked, head_grad, gain).reshape(steps + 1, share, features)
    cotangent = head_back[steps]
    mixed_lows = []
    for position in reversed(range(steps)):
        hidden_grad = jnp.dot(
            cotangent.astype(jnp.bfloat16), full_out, preferred_element_type=jnp.float32
        )
        sigmoid_val = jax.nn.sigmoid(preacts[position])
        preact_grad = (
            hidden_grad * sigmoid_val * (1.0 + preacts[position] * (1.0 - sigmoid_val))
        ).astype(jnp.bfloat16)
        normed_grad = cols_product(preact_grad, full_in)
        mixed_grad = cotangent + norm_back(mixeds[position], normed_grad, gain)
        mixed_lows.append(mixed_grad.astype(jnp.bfloat16))
        cotangent = mixed_grad + head_back[position]
    grad_embed = rows_product(
        jnp.concatenate(onehots[::-1], axis=0), jnp.concatenate(mixed_lows, axis=0)
    )
    rows_embed = num_actions // tables
    embed_sum = sum_over_tables(grad_embed.reshape(tables, rows_embed * features // 128, 128), tables)
    packed = jnp.concatenate([pol_val.reshape(-1, 128), embed_sum], axis=0)
    lines = [[t * members + m for m in range(members)] for t in range(tables)]
    packed = lax.psum(packed, ("table", "mp"), axis_index_groups=lines)
    cut = pol_val.size // 128
    pol_val = packed[:cut].reshape(rows_pol, num_actions + 128)
    out_embed = packed[cut:].reshape(rows_embed, features)
    return pol_val[:, :num_actions], out_embed, pol_val[:, num_actions]


def solution(mesh):
    return jax.shard_map(
        per_device,
        mesh=mesh,
        in_specs=(
            P("table", None),
            P("table", None, None),
            P("table", None),
            P(None, "table"),
            P(None, "table"),
            P("table", "mp"),
            P("table", "mp"),
            P(),
            P(),
            P(),
            P(),
        ),
        out_specs=(P("table", None), P("table", None), P("table")),
        check_vma=False,
    )
```

```python
import functools
import jax
import jax.numpy as jnp
from jax import lax
from jax.experimental import pallas as pl
from jax.experimental.pallas import tpu as pltpu
from jax.sharding import PartitionSpec as P

discount = 0.997
epsilon = 1e-06
f32 = jnp.float32
bf16 = jnp.bfloat16


def dot_nn(a, b):
    return lax.dot_general(a, b, (((1,), (0,)), ((), ())), preferred_element_type=f32)


def dot_nt(a, b):
    return lax.dot_general(a, b, (((1,), (1,)), ((), ())), preferred_element_type=f32)


def inverse_scale(vector):
    return lax.rsqrt(jnp.mean(vector * vector, axis=-1, keepdims=True) + epsilon)


def norm_back(vector, upstream, gain):
    factor = inverse_scale(vector)
    unit_vec = vector * factor
    scaled = upstream * gain
    return factor * (scaled - unit_vec * jnp.mean(scaled * unit_vec, axis=-1, keepdims=True))


def block_kernel(
    steps, share, half, nblocks, arrays, pieces,
    core_ref, obs_ref, emb_ref, keys_ref, targets_ref, value_targets_ref, weight_ref, w_pol_ref,
    w_val_ref, gain_ref, *rest,
):
    hbm = rest[:arrays]
    mine_ref, other_ref = rest[arrays:arrays + 2]
    weights, latents, mixeds, preacts, lows, head_sums, sems = rest[arrays + 2:]
    chips = mine_ref.shape[0]
    core = core_ref[0]
    width = lows.shape[1]
    parts = lows.shape[0] // (steps * share)
    copies = []
    for j, (array, start) in enumerate(pieces):
        source = hbm[array].at[pl.ds(start, weights.shape[1]), :]
        copies.append(pltpu.make_async_copy(source, weights.at[j], sems.at[j]))
        copies[j].start()
    gain = gain_ref[...]

    def rows_of(position):
        return pl.ds(pl.multiple_of(position * share, share), share)

    def forward(position, latent):
        here = rows_of(position)
        mixed = latent + emb_ref[here, :].astype(f32)
        mixeds[here, :] = mixed
        normed = (mixed * inverse_scale(mixed) * gain).astype(bf16)
        total = jnp.zeros_like(mixed)
        for j in range(nblocks):
            @pl.when(position == 0)
            def _():
                copies[j].wait()
            preact = dot_nn(normed, weights[j, :, :half])
            preacts[here, j * half:(j + 1) * half] = preact
            hidden = (preact / (1.0 + jnp.exp(-preact))).astype(bf16)
            total = total + dot_nt(hidden, weights[j, :, half:])
        latent = mixed + total
        latents[rows_of(position + 1), :] = latent
        return latent

    first = obs_ref[...].astype(f32)
    latents[:share, :] = first
    lax.fori_loop(0, steps, forward, first)

    stacked = latents[...]
    scale = inverse_scale(stacked)
    head_in = (stacked * scale * gain).astype(bf16)
    logits = dot_nn(head_in, w_pol_ref[...])
    w_val = w_val_ref[...].astype(f32)
    values = jnp.sum(head_in.astype(f32) * w_val, axis=-1, keepdims=True)
    weight = weight_ref[...]
    exped = jnp.exp(logits - jnp.max(logits, axis=-1, keepdims=True))
    probs = exped / jnp.sum(exped, axis=-1, keepdims=True)
    logit_grad = (weight * (probs - targets_ref[...])).astype(bf16)
    value_grad = 2.0 * weight * (values - value_targets_ref[...])
    high = value_grad.astype(bf16)
    low = (value_grad - high.astype(f32)).astype(bf16)
    lane = lax.broadcasted_iota(jnp.int32, (value_grad.shape[0], 128), 1)
    value_lanes = jnp.where(lane == 0, high, jnp.where(lane == 1, low, jnp.zeros_like(low)))
    head_grads = jnp.concatenate([logit_grad, value_lanes], axis=1)
    sums = lax.dot_general(
        head_in, head_grads, (((0,), (0,)), ((), ())), preferred_element_type=f32
    )
    head_sums[...] = sums.reshape(head_sums.shape)
    columns = sums.shape[1]
    mine_ref[:, :, :columns] = head_sums[:, core]
    other_ref[:, :, :columns] = head_sums[:, 1 - core].astype(bf16)
    head_grad = dot_nt(logit_grad, w_pol_ref[...]) + value_grad * w_val
    unit_vec = stacked * scale
    scaled = head_grad * gain
    latents[...] = scale * (scaled - unit_vec * jnp.mean(scaled * unit_vec, axis=-1, keepdims=True))

    def backward(index, cotangent):
        position = steps - 1 - index
        here = rows_of(position)
        low = cotangent.astype(bf16)
        total = jnp.zeros_like(cotangent)
        for j in range(nblocks):
            hidden_grad = dot_nn(low, weights[j, :, half:])
            preact = preacts[here, j * half:(j + 1) * half]
            sig = 1.0 / (1.0 + jnp.exp(-preact))
            preact_grad = (hidden_grad * sig * (1.0 + preact * (1.0 - sig))).astype(bf16)
            total = total + dot_nt(preact_grad, weights[j, :, :half])
        mixed_grad = cotangent + norm_back(mixeds[here, :], total, gain)
        mixed_low = mixed_grad.astype(bf16)
        for quarter in range(parts):
            start = pl.multiple_of(quarter * steps * share + position * share, share)
            lows[pl.ds(start, share), :] = mixed_low[:, quarter * width:(quarter + 1) * width]
        return mixed_grad + latents[here, :]

    lax.fori_loop(0, steps, backward, latents[steps * share:, :])

    row = lax.broadcasted_iota(jnp.int32, (chips * 8, keys_ref.shape[1]), 0)
    row_key = 2 * row - (row & 7)
    for side, target in ((core, mine_ref), (1 - core, other_ref)):
        picks = jnp.where(row_key + 8 * side == keys_ref[...], 1.0, 0.0).astype(bf16)
        summed = dot_nn(picks, lows[...]).reshape(chips, 8, width)
        target[:, :, columns:] = summed.astype(target.dtype)


def run_block(
    core, obs0, emb, actions, targets, value_targets, weight, w_pol, w_val, gain, blocks, chips
):
    share, features = obs0.shape
    steps = emb.shape[0] // share
    num_actions = w_pol.shape[1]
    parts = 8 * chips * 2 // num_actions
    width = features // parts
    columns = num_actions + 128 + width
    quarters = jnp.arange(parts, dtype=jnp.int32)
    keys = (actions.reshape(1, -1) * parts + quarters[:, None]).reshape(1, -1)
    nblocks = sum(block.shape[0] for block in blocks) // features
    half = blocks[0].shape[1] // 2
    rows = (steps + 1) * share
    pieces = [
        (i, k * features) for i, block in enumerate(blocks) for k in range(block.shape[0] // features)
    ]
    vmem = pl.BlockSpec(memory_space=pltpu.VMEM)
    return pl.pallas_call(
        functools.partial(block_kernel, steps, share, half, nblocks, len(blocks), tuple(pieces)),
        out_shape=(
            jax.ShapeDtypeStruct((chips, 8, columns), f32),
            jax.ShapeDtypeStruct((chips, 8, columns), bf16),
        ),
        in_specs=[pl.BlockSpec(memory_space=pltpu.SMEM)]
        + [vmem] * 9
        + [pl.BlockSpec(memory_space=pltpu.HBM)] * len(blocks),
        out_specs=(vmem,) * 2,
        scratch_shapes=[
            pltpu.VMEM((nblocks, features, 2 * half), bf16),
            pltpu.VMEM((rows, features), f32),
            pltpu.VMEM((steps * share, features), f32),
            pltpu.VMEM((steps * share, nblocks * half), f32),
            pltpu.VMEM((parts * steps * share, width), bf16),
            pltpu.VMEM((chips, 2, 8, num_actions + 128), f32),
            pltpu.SemaphoreType.DMA((nblocks,)),
        ],
        compiler_params=pltpu.CompilerParams(vmem_limit_bytes=40 * 1024 * 1024),
        cost_estimate=pl.CostEstimate(flops=3 * 10**9, bytes_accessed=10**7, transcendentals=0),
    )(core, obs0, emb, keys, targets, value_targets, weight, w_pol, w_val, gain, *blocks)


def cores_swap(value, tables):
    return lax.ppermute(value, "table", [(t, t ^ 1) for t in range(tables)])


def along_x(value, step, members):
    return lax.ppermute(value, "mp", [(m, (m + step) % members) for m in range(members)])


def same_core_groups(tables):
    return [[2 * k + c for k in range(tables // 2)] for c in range(2)]


def own_rows_of_weights(w_in, w_out, core, tables):
    half = w_in.shape[1] // 2
    low = jnp.concatenate([w_in[:, :half], w_out[:, :half]], axis=1)
    high = jnp.concatenate([w_in[:, half:], w_out[:, half:]], axis=1)
    first = core == 0
    mine = jnp.where(first, low, high)
    got = cores_swap(jnp.where(first, high, low), tables)
    return jnp.where(
        first, jnp.concatenate([mine, got], axis=0), jnp.concatenate([got, mine], axis=0)
    )


def gather_plane(rows, tables):
    return lax.all_to_all(
        jnp.tile(rows, (tables // 2, 1)),
        "table",
        split_axis=0,
        concat_axis=0,
        tiled=True,
        axis_index_groups=same_core_groups(tables),
    )


def gather_blocks(own, tables, members):
    groups = [
        [(2 * k + c) * members + m for c in range(2) for m in range(members)]
        for k in range(tables // 2)
    ]
    return [lax.all_gather(own, ("table", "mp"), axis=0, tiled=True, axis_index_groups=groups)]


def pick_unrolls(replay, request_rows, request_count, steps, member, tables, members):
    share = tables // members
    width = replay.shape[1]
    firsts = request_rows[0, :, 0].reshape(share, members)
    firsts = lax.dynamic_index_in_dim(firsts, member, 1, keepdims=False)
    counts = lax.dynamic_index_in_dim(
        request_count[0].reshape(share, members), member, 1, keepdims=False
    )
    used = (counts > 0).astype(f32)
    offsets = jnp.arange(8, dtype=jnp.int32)
    positions = firsts[:, None] + offsets[None, :]
    row_ids = jnp.arange(replay.shape[0], dtype=jnp.int32)
    picks = (positions.reshape(-1)[:, None] == row_ids[None, :]).astype(bf16)
    rows = jnp.dot(picks, replay, preferred_element_type=f32).reshape(share, 8, width)
    rows = jnp.where(offsets[None, :, None] <= steps, rows, used[:, None, None])
    return rows.astype(bf16)


def swap_digits(rows, tables, members):
    share = tables // members
    swap = [
        ((members * a + b) * members + d, (members * a + d) * members + b)
        for a in range(share)
        for b in range(members)
        for d in range(members)
    ]
    return lax.ppermute(rows, ("table", "mp"), swap)


def deliver_unrolls(rows, tables, members):
    share = tables // members
    groups = [[members * a + d for a in range(share)] for d in range(members)]
    return lax.all_to_all(
        rows, "table", split_axis=0, concat_axis=0, tiled=True, axis_index_groups=groups
    )


def reduce_partials(mine, other, tables, members):
    got = cores_swap(other, tables)
    summed = (mine + got.astype(f32)).astype(bf16)
    parts = lax.all_to_all(
        summed,
        "table",
        split_axis=0,
        concat_axis=0,
        tiled=True,
        axis_index_groups=same_core_groups(tables),
    )
    summed = jnp.sum(parts.astype(f32), axis=0)
    copies = jnp.broadcast_to(summed[None], (members, *summed.shape))
    return jnp.sum(lax.all_to_all(copies, "mp", split_axis=0, concat_axis=0, tiled=True), axis=0)


def per_device(
    replay, request_rows, request_count, actions, rewards, w_in, w_out, w_pol, w_val, embed, gain
):
    tables = lax.axis_size("table")
    members = lax.axis_size("mp")
    member = lax.axis_index("mp")
    core = lax.axis_index("table") % 2
    share = tables // members
    features = replay.shape[1]
    steps = actions.shape[0]
    num_actions = w_pol.shape[1]
    own_rows = own_rows_of_weights(w_in, w_out, core, tables)
    rows = pick_unrolls(replay, request_rows, request_count, steps, member, tables, members)
    own = gather_plane(own_rows, tables)
    blocks = gather_blocks(own, tables, members)
    rows, _ = lax.optimization_barrier((rows, own))
    rows = swap_digits(rows, tables, members)
    rows = deliver_unrolls(rows, tables, members)
    observed = rows[:, : steps + 1].transpose(1, 0, 2)
    used_rows = rows[:, steps + 1, 0].astype(f32)
    actions = lax.dynamic_index_in_dim(
        actions.reshape(steps, share, members), member, 2, keepdims=False
    )
    rewards = lax.dynamic_index_in_dim(
        rewards.reshape(steps, share, members), member, 2, keepdims=False
    )
    flat_obs = observed.reshape((steps + 1) * share, features).astype(f32)
    target_in = (flat_obs * inverse_scale(flat_obs) * gain).astype(bf16)
    target_logits = jnp.dot(target_in, w_pol, preferred_element_type=f32)
    target_values = jnp.dot(target_in, w_val, preferred_element_type=f32).reshape(
        steps + 1, share
    )
    policy_targets = jax.nn.softmax(target_logits, axis=-1)
    value_targets = jnp.concatenate(
        [rewards + discount * target_values[1:], target_values[steps:]], axis=0
    )
    action_ids = jnp.arange(num_actions, dtype=jnp.int32)
    onehots = (actions.reshape(-1)[:, None] == action_ids[None, :]).astype(bf16)
    emb = jnp.dot(onehots, embed, preferred_element_type=f32).astype(bf16)
    row_weight = jnp.tile(used_rows / tables, steps + 1)
    mine, other = run_block(
        core.reshape(1),
        observed[0],
        emb,
        actions,
        policy_targets,
        value_targets.reshape(-1, 1),
        row_weight[:, None],
        w_pol,
        w_val[None, :],
        gain[None, :],
        blocks,
        tables // 2,
    )
    rows = reduce_partials(mine, other, tables, members)
    out_pol = rows[:, :num_actions]
    out_val = rows[:, num_actions] + rows[:, num_actions + 1]
    out_embed = rows[:, num_actions + 128 :].reshape(num_actions // tables, features)
    return out_pol, out_embed, out_val


def solution(mesh):
    return jax.shard_map(
        per_device,
        mesh=mesh,
        in_specs=(
            P("table", None),
            P("table", None, None),
            P("table", None),
            P(None, "table"),
            P(None, "table"),
            P("table", "mp"),
            P("table", "mp"),
            P(),
            P(),
            P(),
            P(),
        ),
        out_specs=(P("table", None), P("table", None), P("table")),
        check_vma=False,
    )
```

```python
import functools
import jax
import jax.numpy as jnp
from jax import lax
from jax.experimental import pallas as pl
from jax.experimental.pallas import tpu as pltpu
from jax.sharding import PartitionSpec as P

discount = 0.997
epsilon = 1e-06
f32 = jnp.float32
bf16 = jnp.bfloat16


def dot_nn(a, b):
    return lax.dot_general(a, b, (((1,), (0,)), ((), ())), preferred_element_type=f32)


def dot_nt(a, b):
    return lax.dot_general(a, b, (((1,), (1,)), ((), ())), preferred_element_type=f32)


def inverse_scale(vector):
    return lax.rsqrt(jnp.mean(vector * vector, axis=-1, keepdims=True) + epsilon)


def norm_back(vector, upstream, gain):
    factor = inverse_scale(vector)
    unit_vec = vector * factor
    scaled = upstream * gain
    return factor * (scaled - unit_vec * jnp.mean(scaled * unit_vec, axis=-1, keepdims=True))


def block_kernel(
    steps, share, half, nblocks, arrays, pieces,
    core_ref, obs_ref, emb_ref, keys_ref, targets_ref, value_targets_ref, weight_ref, w_pol_ref,
    w_val_ref, gain_ref, *rest,
):
    hbm = rest[:arrays]
    mine_ref, other_ref = rest[arrays:arrays + 2]
    weights, latents, mixeds, slopes, lows, head_sums, sems = rest[arrays + 2:]
    chips = mine_ref.shape[0]
    core = core_ref[0]
    width = lows.shape[1]
    parts = lows.shape[0] // (steps * share)
    copies = []
    for j, (array, start) in enumerate(pieces):
        source = hbm[array].at[pl.ds(start, weights.shape[1]), :]
        copies.append(pltpu.make_async_copy(source, weights.at[j], sems.at[j]))
        copies[j].start()
    gain = gain_ref[...]

    def rows_of(position):
        start = position * share
        return pl.ds(start if isinstance(start, int) else pl.multiple_of(start, share), share)

    def forward(position, latent, arriving=False):
        here = rows_of(position)
        mixed = latent + emb_ref[here, :].astype(f32)
        mixeds[here, :] = mixed
        normed = (mixed * inverse_scale(mixed) * gain).astype(bf16)
        hiddens = []
        for j in range(nblocks):
            if arriving:
                copies[j].wait()
            preact = dot_nn(normed, weights[j, :, :half])
            sig = 1.0 / (1.0 + jnp.exp(-preact))
            slopes[here, j * half:(j + 1) * half] = sig * (1.0 + preact * (1.0 - sig))
            hiddens.append((preact * sig).astype(bf16))
        total = jnp.zeros((mixed.shape[1], share), f32)
        for j in range(nblocks):
            total = total + dot_nt(weights[j, :, half:], hiddens[j])
        total = total.T
        latent = mixed + total
        latents[rows_of(position + 1), :] = latent
        return latent

    first = obs_ref[...].astype(f32)
    latents[:share, :] = first
    lax.fori_loop(1, steps, forward, forward(0, first, arriving=True))

    stacked = latents[...]
    scale = inverse_scale(stacked)
    head_in = (stacked * scale * gain).astype(bf16)
    logits = dot_nn(head_in, w_pol_ref[...])
    w_val = w_val_ref[...].astype(f32)
    values = jnp.sum(head_in.astype(f32) * w_val, axis=-1, keepdims=True)
    weight = weight_ref[...]
    exped = jnp.exp(logits - jnp.max(logits, axis=-1, keepdims=True))
    probs = exped / jnp.sum(exped, axis=-1, keepdims=True)
    logit_grad = (weight * (probs - targets_ref[...])).astype(bf16)
    value_grad = 2.0 * weight * (values - value_targets_ref[...])
    high = value_grad.astype(bf16)
    low = (value_grad - high.astype(f32)).astype(bf16)
    lane = lax.broadcasted_iota(jnp.int32, (value_grad.shape[0], 128), 1)
    value_lanes = jnp.where(lane == 0, high, jnp.where(lane == 1, low, jnp.zeros_like(low)))
    head_grads = jnp.concatenate([logit_grad, value_lanes], axis=1)
    sums = lax.dot_general(
        head_in, head_grads, (((0,), (0,)), ((), ())), preferred_element_type=f32
    )
    head_sums[...] = sums.reshape(head_sums.shape)
    columns = sums.shape[1]
    mine_ref[:, :, :columns] = head_sums[:, core]
    other_ref[:, :, :columns] = head_sums[:, 1 - core].astype(bf16)
    head_grad = dot_nt(logit_grad, w_pol_ref[...]) + value_grad * w_val
    unit_vec = stacked * scale
    scaled = head_grad * gain
    latents[...] = scale * (scaled - unit_vec * jnp.mean(scaled * unit_vec, axis=-1, keepdims=True))

    def backward(index, cotangent):
        position = steps - 1 - index
        here = rows_of(position)
        low = cotangent.astype(bf16)
        preact_grads = []
        for j in range(nblocks):
            hidden_grad = dot_nn(low, weights[j, :, half:])
            preact_grads.append((hidden_grad * slopes[here, j * half:(j + 1) * half]).astype(bf16))
        total = jnp.zeros((cotangent.shape[1], share), f32)
        for j in range(nblocks):
            total = total + dot_nt(weights[j, :, :half], preact_grads[j])
        total = total.T
        mixed_grad = cotangent + norm_back(mixeds[here, :], total, gain)
        mixed_low = mixed_grad.astype(bf16)
        for quarter in range(parts):
            start = pl.multiple_of(quarter * steps * share + position * share, share)
            lows[pl.ds(start, share), :] = mixed_low[:, quarter * width:(quarter + 1) * width]
        return mixed_grad + latents[here, :]

    lax.fori_loop(0, steps, backward, latents[steps * share:, :])

    row = lax.broadcasted_iota(jnp.int32, (chips * 8, keys_ref.shape[1]), 0)
    row_key = 2 * row - (row & 7)
    for side, target in ((core, mine_ref), (1 - core, other_ref)):
        picks = jnp.where(row_key + 8 * side == keys_ref[...], 1.0, 0.0).astype(bf16)
        summed = dot_nn(picks, lows[...]).reshape(chips, 8, width)
        target[:, :, columns:] = summed.astype(target.dtype)


def run_block(
    core, obs0, emb, actions, targets, value_targets, weight, w_pol, w_val, gain, blocks, chips
):
    share, features = obs0.shape
    steps = emb.shape[0] // share
    num_actions = w_pol.shape[1]
    parts = 8 * chips * 2 // num_actions
    width = features // parts
    columns = num_actions + 128 + width
    quarters = jnp.arange(parts, dtype=jnp.int32)
    keys = (actions.reshape(1, -1) * parts + quarters[:, None]).reshape(1, -1)
    nblocks = sum(block.shape[0] for block in blocks) // features
    half = blocks[0].shape[1] // 2
    rows = (steps + 1) * share
    pieces = [
        (i, k * features) for i, block in enumerate(blocks) for k in range(block.shape[0] // features)
    ]
    vmem = pl.BlockSpec(memory_space=pltpu.VMEM)
    return pl.pallas_call(
        functools.partial(block_kernel, steps, share, half, nblocks, len(blocks), tuple(pieces)),
        out_shape=(
            jax.ShapeDtypeStruct((chips, 8, columns), f32),
            jax.ShapeDtypeStruct((chips, 8, columns), bf16),
        ),
        in_specs=[pl.BlockSpec(memory_space=pltpu.SMEM)]
        + [vmem] * 9
        + [pl.BlockSpec(memory_space=pltpu.HBM)] * len(blocks),
        out_specs=(vmem,) * 2,
        scratch_shapes=[
            pltpu.VMEM((nblocks, features, 2 * half), bf16),
            pltpu.VMEM((rows, features), f32),
            pltpu.VMEM((steps * share, features), f32),
            pltpu.VMEM((steps * share, nblocks * half), f32),
            pltpu.VMEM((parts * steps * share, width), bf16),
            pltpu.VMEM((chips, 2, 8, num_actions + 128), f32),
            pltpu.SemaphoreType.DMA((nblocks,)),
        ],
        compiler_params=pltpu.CompilerParams(vmem_limit_bytes=57 * 1024 * 1024),
        cost_estimate=pl.CostEstimate(flops=3 * 10**9, bytes_accessed=10**7, transcendentals=0),
    )(core, obs0, emb, keys, targets, value_targets, weight, w_pol, w_val, gain, *blocks)


def cores_swap(value, tables):
    return lax.ppermute(value, "table", [(t, t ^ 1) for t in range(tables)])


def along_x(value, step, members):
    return lax.ppermute(value, "mp", [(m, (m + step) % members) for m in range(members)])


def same_core_groups(tables):
    return [[2 * k + c for k in range(tables // 2)] for c in range(2)]


def own_rows_of_weights(w_in, w_out, core, tables):
    half = w_in.shape[1] // 2
    low = jnp.concatenate([w_in[:, :half], w_out[:, :half]], axis=1)
    high = jnp.concatenate([w_in[:, half:], w_out[:, half:]], axis=1)
    first = core == 0
    mine = jnp.where(first, low, high)
    got = cores_swap(jnp.where(first, high, low), tables)
    return jnp.where(
        first, jnp.concatenate([mine, got], axis=0), jnp.concatenate([got, mine], axis=0)
    )


def gather_plane(rows, tables):
    return lax.all_to_all(
        jnp.tile(rows, (tables // 2, 1)),
        "table",
        split_axis=0,
        concat_axis=0,
        tiled=True,
        axis_index_groups=same_core_groups(tables),
    )


def gather_blocks(own, tables, members):
    groups = [
        [(2 * k + c) * members + m for c in range(2) for m in range(members)]
        for k in range(tables // 2)
    ]
    return [lax.all_gather(own, ("table", "mp"), axis=0, tiled=True, axis_index_groups=groups)]


def pick_unrolls(replay, request_rows, request_count, steps, member, tables, members):
    share = tables // members
    width = replay.shape[1]
    firsts = request_rows[0, :, 0].reshape(share, members)
    firsts = lax.dynamic_index_in_dim(firsts, member, 1, keepdims=False)
    counts = lax.dynamic_index_in_dim(
        request_count[0].reshape(share, members), member, 1, keepdims=False
    )
    used = (counts > 0).astype(f32)
    offsets = jnp.arange(8, dtype=jnp.int32)
    positions = firsts[:, None] + offsets[None, :]
    row_ids = jnp.arange(replay.shape[0], dtype=jnp.int32)
    picks = (positions.reshape(-1)[:, None] == row_ids[None, :]).astype(bf16)
    rows = jnp.dot(picks, replay, preferred_element_type=f32).reshape(share, 8, width)
    rows = jnp.where(offsets[None, :, None] <= steps, rows, used[:, None, None])
    return rows.astype(bf16)


def swap_digits(rows, tables, members):
    share = tables // members
    swap = [
        ((members * a + b) * members + d, (members * a + d) * members + b)
        for a in range(share)
        for b in range(members)
        for d in range(members)
    ]
    return lax.ppermute(rows, ("table", "mp"), swap)


def deliver_unrolls(rows, tables, members):
    share = tables // members
    groups = [[members * a + d for a in range(share)] for d in range(members)]
    return lax.all_to_all(
        rows, "table", split_axis=0, concat_axis=0, tiled=True, axis_index_groups=groups
    )


def reduce_partials(mine, other, tables, members):
    got = cores_swap(other, tables)
    summed = (mine + got.astype(f32)).astype(bf16)
    parts = lax.all_to_all(
        summed,
        "table",
        split_axis=0,
        concat_axis=0,
        tiled=True,
        axis_index_groups=same_core_groups(tables),
    )
    summed = jnp.sum(parts.astype(f32), axis=0)
    copies = jnp.broadcast_to(summed[None], (members, *summed.shape))
    return jnp.sum(lax.all_to_all(copies, "mp", split_axis=0, concat_axis=0, tiled=True), axis=0)


def per_device(
    replay, request_rows, request_count, actions, rewards, w_in, w_out, w_pol, w_val, embed, gain
):
    tables = lax.axis_size("table")
    members = lax.axis_size("mp")
    member = lax.axis_index("mp")
    core = lax.axis_index("table") % 2
    share = tables // members
    features = replay.shape[1]
    steps = actions.shape[0]
    num_actions = w_pol.shape[1]
    own_rows = own_rows_of_weights(w_in, w_out, core, tables)
    rows = pick_unrolls(replay, request_rows, request_count, steps, member, tables, members)
    own = gather_plane(own_rows, tables)
    blocks = gather_blocks(own, tables, members)
    rows, _ = lax.optimization_barrier((rows, own))
    rows = swap_digits(rows, tables, members)
    rows = deliver_unrolls(rows, tables, members)
    observed = rows[:, : steps + 1].transpose(1, 0, 2)
    used_rows = rows[:, steps + 1, 0].astype(f32)
    actions = lax.dynamic_index_in_dim(
        actions.reshape(steps, share, members), member, 2, keepdims=False
    )
    rewards = lax.dynamic_index_in_dim(
        rewards.reshape(steps, share, members), member, 2, keepdims=False
    )
    flat_obs = observed.reshape((steps + 1) * share, features).astype(f32)
    target_in = (flat_obs * inverse_scale(flat_obs) * gain).astype(bf16)
    target_logits = jnp.dot(target_in, w_pol, preferred_element_type=f32)
    target_values = jnp.dot(target_in, w_val, preferred_element_type=f32).reshape(
        steps + 1, share
    )
    policy_targets = jax.nn.softmax(target_logits, axis=-1)
    value_targets = jnp.concatenate(
        [rewards + discount * target_values[1:], target_values[steps:]], axis=0
    )
    action_ids = jnp.arange(num_actions, dtype=jnp.int32)
    onehots = (actions.reshape(-1)[:, None] == action_ids[None, :]).astype(bf16)
    emb = jnp.dot(onehots, embed, preferred_element_type=f32).astype(bf16)
    row_weight = jnp.tile(used_rows / tables, steps + 1)
    mine, other = run_block(
        core.reshape(1),
        observed[0],
        emb,
        actions,
        policy_targets,
        value_targets.reshape(-1, 1),
        row_weight[:, None],
        w_pol,
        w_val[None, :],
        gain[None, :],
        blocks,
        tables // 2,
    )
    rows = reduce_partials(mine, other, tables, members)
    out_pol = rows[:, :num_actions]
    out_val = rows[:, num_actions] + rows[:, num_actions + 1]
    out_embed = rows[:, num_actions + 128 :].reshape(num_actions // tables, features)
    return out_pol, out_embed, out_val


def solution(mesh):
    return jax.shard_map(
        per_device,
        mesh=mesh,
        in_specs=(
            P("table", None),
            P("table", None, None),
            P("table", None),
            P(None, "table"),
            P(None, "table"),
            P("table", "mp"),
            P("table", "mp"),
            P(),
            P(),
            P(),
            P(),
        ),
        out_specs=(P("table", None), P("table", None), P("table")),
        check_vma=False,
    )
```

```python
import functools
import jax
import jax.numpy as jnp
from jax import lax
from jax.experimental import pallas as pl
from jax.experimental.pallas import tpu as pltpu
from jax.sharding import PartitionSpec as P

discount = 0.997
epsilon = 1e-06
f32 = jnp.float32
bf16 = jnp.bfloat16


def dot_nn(a, b):
    return lax.dot_general(a, b, (((1,), (0,)), ((), ())), preferred_element_type=f32)


def dot_nt(a, b):
    return lax.dot_general(a, b, (((1,), (1,)), ((), ())), preferred_element_type=f32)


def inverse_scale(vector):
    return lax.rsqrt(jnp.mean(vector * vector, axis=-1, keepdims=True) + epsilon)


def norm_back(vector, upstream, gain):
    factor = inverse_scale(vector)
    unit_vec = vector * factor
    scaled = upstream * gain
    return factor * (scaled - unit_vec * jnp.mean(scaled * unit_vec, axis=-1, keepdims=True))


def block_kernel(
    steps, share, lines, halves,
    weights_hbm, unorder_hbm, core_ref, start_ref, keys_ref, targets_ref, value_targets_ref, weight_ref, w_pol_ref,
    w_val_ref, gain_ref, mine_ref, other_ref, weights, unorder, latents, mixeds, slopes, mixed_lows,
    lows, head_sums, sems,
):
    chips = mine_ref.shape[0]
    core = core_ref[0]
    width = lows.shape[1]
    parts = lows.shape[0] // (steps * share)
    depth, units = weights.shape[1], weights.shape[2] // 2
    spans = [slice(side * depth, (side + 1) * depth) for side in range(halves)]
    copies = [
        [
            pltpu.make_async_copy(
                weights_hbm.at[pl.ds((side * lines + line) * depth, depth), :],
                weights.at[side * lines + line],
                sems.at[side * lines + line],
            )
            for side in range(halves)
        ]
        for line in range(lines)
    ]
    for line_copies in copies:
        for copy in line_copies:
            copy.start()
    unorder_copy = pltpu.make_async_copy(unorder_hbm, unorder, sems.at[halves * lines])
    unorder_copy.start()
    gain = gain_ref[...]

    def rows_of(position):
        start = position * share
        return pl.ds(start if isinstance(start, int) else pl.multiple_of(start, share), share)

    def forward(position, latent, arriving=False):
        here = rows_of(position)
        mixed = latent + start_ref[here, :].astype(f32)
        mixeds[here, :] = mixed
        normed = (mixed * inverse_scale(mixed) * gain).astype(bf16)
        hiddens = []
        for line in range(lines):
            if arriving:
                for copy in copies[line]:
                    copy.wait()
            preact = sum(
                dot_nn(normed[:, span], weights[side * lines + line, :, :units])
                for side, span in enumerate(spans)
            )
            sig = 1.0 / (1.0 + jnp.exp(-preact))
            slopes[here, line * units:(line + 1) * units] = sig * (1.0 + preact * (1.0 - sig))
            hiddens.append((preact * sig).astype(bf16))
        total = jnp.concatenate(
            [
                sum(
                    dot_nt(weights[side * lines + line, :, units:], hiddens[line])
                    for line in range(lines)
                )
                for side in range(halves)
            ],
            axis=0,
        ).T
        latent = mixed + total
        latents[rows_of(position + 1), :] = latent
        return latent

    first = start_ref[steps * share:, :].astype(f32)
    latents[:share, :] = first
    lax.fori_loop(1, steps, forward, forward(0, first, arriving=True))

    stacked = latents[...]
    scale = inverse_scale(stacked)
    head_in = (stacked * scale * gain).astype(bf16)
    logits = dot_nn(head_in, w_pol_ref[...])
    w_val = w_val_ref[...].astype(f32)
    values = jnp.sum(head_in.astype(f32) * w_val, axis=-1, keepdims=True)
    weight = weight_ref[...]
    exped = jnp.exp(logits - jnp.max(logits, axis=-1, keepdims=True))
    probs = exped / jnp.sum(exped, axis=-1, keepdims=True)
    logit_grad = (weight * (probs - targets_ref[...])).astype(bf16)
    value_grad = 2.0 * weight * (values - value_targets_ref[...])
    high = value_grad.astype(bf16)
    low = (value_grad - high.astype(f32)).astype(bf16)
    lane = lax.broadcasted_iota(jnp.int32, (value_grad.shape[0], 128), 1)
    value_lanes = jnp.where(lane == 0, high, jnp.where(lane == 1, low, jnp.zeros_like(low)))
    head_grads = jnp.concatenate([logit_grad, value_lanes], axis=1)
    sums = lax.dot_general(
        head_in, head_grads, (((0,), (0,)), ((), ())), preferred_element_type=f32
    )
    head_sums[...] = sums.reshape(head_sums.shape)
    columns = sums.shape[1]
    mine_ref[:, :, :columns] = head_sums[core].astype(bf16)
    other_ref[:, :, :columns] = head_sums[1 - core].astype(bf16)
    head_grad = dot_nt(logit_grad, w_pol_ref[...]) + value_grad * w_val
    unit_vec = stacked * scale
    scaled = head_grad * gain
    latents[...] = scale * (scaled - unit_vec * jnp.mean(scaled * unit_vec, axis=-1, keepdims=True))

    def backward(index, cotangent):
        position = steps - 1 - index
        here = rows_of(position)
        low = cotangent.astype(bf16)
        preact_grads = []
        for line in range(lines):
            hidden_grad = sum(
                dot_nn(low[:, span], weights[side * lines + line, :, units:])
                for side, span in enumerate(spans)
            )
            slope = slopes[here, line * units:(line + 1) * units]
            preact_grads.append((hidden_grad * slope).astype(bf16))
        total = jnp.concatenate(
            [
                sum(
                    dot_nt(weights[side * lines + line, :, :units], preact_grads[line])
                    for line in range(lines)
                )
                for side in range(halves)
            ],
            axis=0,
        ).T
        mixed_grad = cotangent + norm_back(mixeds[here, :], total, gain)
        mixed_lows[here, :] = mixed_grad.astype(bf16)
        return mixed_grad + latents[here, :]

    lax.fori_loop(0, steps, backward, latents[steps * share:, :])

    unorder_copy.wait()
    for quarter in range(parts):
        quarter_lows = dot_nn(mixed_lows[...], unorder[:, quarter * width:(quarter + 1) * width])
        lows[quarter * steps * share:(quarter + 1) * steps * share, :] = quarter_lows.astype(bf16)
    row = lax.broadcasted_iota(jnp.int32, (chips * 8, keys_ref.shape[1]), 0)
    row_key = 2 * row - (row & 7)
    for side, target in ((core, mine_ref), (1 - core, other_ref)):
        picks = jnp.where(row_key + 8 * side == keys_ref[...], 1.0, 0.0).astype(bf16)
        summed = dot_nn(picks, lows[...]).reshape(chips, 8, width)
        target[:, :, columns:] = summed.astype(target.dtype)


def run_block(
    core, starts, actions, targets, value_targets, weight, w_pol, w_val, gain, blocks, unorder, chips
):
    steps, share = actions.shape
    features = starts.shape[1]
    halves = 2
    depth = features // halves
    units = blocks.shape[1] // 2
    lines = blocks.shape[0] // features
    rows = (steps + 1) * share
    num_actions = w_pol.shape[1]
    parts = 8 * chips * 2 // num_actions
    width = features // parts
    columns = num_actions + 128 + width
    quarters = jnp.arange(parts, dtype=jnp.int32)
    keys = (actions.reshape(1, -1) * parts + quarters[:, None]).reshape(1, -1)
    vmem = pl.BlockSpec(memory_space=pltpu.VMEM)
    return pl.pallas_call(
        functools.partial(block_kernel, steps, share, lines, halves),
        out_shape=(
            jax.ShapeDtypeStruct((chips, 8, columns), bf16),
            jax.ShapeDtypeStruct((chips, 8, columns), bf16),
        ),
        in_specs=[pl.BlockSpec(memory_space=pltpu.HBM)] * 2
        + [pl.BlockSpec(memory_space=pltpu.SMEM)]
        + [vmem] * 8,
        out_specs=(vmem,) * 2,
        scratch_shapes=[
            pltpu.VMEM((halves * lines, depth, 2 * units), bf16),
            pltpu.VMEM((features, features), bf16),
            pltpu.VMEM((rows, features), f32),
            pltpu.VMEM((steps * share, features), f32),
            pltpu.VMEM((steps * share, lines * units), f32),
            pltpu.VMEM((steps * share, features), bf16),
            pltpu.VMEM((parts * steps * share, width), bf16),
            pltpu.VMEM((halves, chips, 8, num_actions + 128), f32),
            pltpu.SemaphoreType.DMA((halves * lines + 1,)),
        ],
        compiler_params=pltpu.CompilerParams(vmem_limit_bytes=57 * 1024 * 1024),
        cost_estimate=pl.CostEstimate(flops=3 * 10**9, bytes_accessed=10**7, transcendentals=0),
    )(blocks, unorder, core, starts, keys, targets, value_targets, weight, w_pol, w_val, gain)


def cores_swap(value, tables):
    return lax.ppermute(value, "table", [(t, t ^ 1) for t in range(tables)])


def along_x(value, step, members):
    return lax.ppermute(value, "mp", [(m, (m + step) % members) for m in range(members)])


def same_core_groups(tables):
    return [[2 * k + c for k in range(tables // 2)] for c in range(2)]


def gather_plane(rows, tables):
    return lax.all_to_all(
        jnp.tile(rows, (tables // 2, 1)),
        "table",
        split_axis=0,
        concat_axis=0,
        tiled=True,
        axis_index_groups=same_core_groups(tables),
    )


def gather_blocks(own, tables, members):
    groups = [
        [(2 * k + c) * members + m for c in range(2) for m in range(members)]
        for k in range(tables // 2)
    ]
    return lax.all_gather(own, ("table", "mp"), axis=0, tiled=True, axis_index_groups=groups)


def pick_unrolls(replay, request_rows, request_count, steps, member, tables, members):
    share = tables // members
    width = replay.shape[1]
    firsts = request_rows[0, :, 0].reshape(share, members)
    firsts = lax.dynamic_index_in_dim(firsts, member, 1, keepdims=False)
    counts = lax.dynamic_index_in_dim(
        request_count[0].reshape(share, members), member, 1, keepdims=False
    )
    used = (counts > 0).astype(f32)
    offsets = jnp.arange(8, dtype=jnp.int32)
    positions = firsts[:, None] + offsets[None, :]
    row_ids = jnp.arange(replay.shape[0], dtype=jnp.int32)
    picks = (positions.reshape(-1)[:, None] == row_ids[None, :]).astype(bf16)
    rows = jnp.dot(picks, replay, preferred_element_type=f32).reshape(share, 8, width)
    rows = jnp.where(offsets[None, :, None] <= steps, rows, used[:, None, None])
    return rows.astype(bf16)


def swap_digits(rows, tables, members):
    share = tables // members
    swap = [
        ((members * a + b) * members + d, (members * a + d) * members + b)
        for a in range(share)
        for b in range(members)
        for d in range(members)
    ]
    return lax.ppermute(rows, ("table", "mp"), swap)


def deliver_unrolls(rows, tables, members):
    share = tables // members
    groups = [[members * a + d for a in range(share)] for d in range(members)]
    return lax.all_to_all(
        rows, "table", split_axis=0, concat_axis=0, tiled=True, axis_index_groups=groups
    )


def reduce_partials(mine, other, tables, members):
    got = cores_swap(other, tables)
    summed = (mine.astype(f32) + got.astype(f32)).astype(bf16)
    parts = lax.all_to_all(
        summed,
        "table",
        split_axis=0,
        concat_axis=0,
        tiled=True,
        axis_index_groups=same_core_groups(tables),
    )
    summed = jnp.sum(parts.astype(f32), axis=0)
    copies = jnp.broadcast_to(summed[None], (members, *summed.shape))
    return jnp.sum(lax.all_to_all(copies, "mp", split_axis=0, concat_axis=0, tiled=True), axis=0)


def per_device(
    replay, request_rows, request_count, actions, rewards, w_in, w_out, w_pol, w_val, embed, gain
):
    tables = lax.axis_size("table")
    members = lax.axis_size("mp")
    member = lax.axis_index("mp")
    core = lax.axis_index("table") % 2
    share = tables // members
    features = replay.shape[1]
    steps = actions.shape[0]
    num_actions = w_pol.shape[1]
    rows = pick_unrolls(replay, request_rows, request_count, steps, member, tables, members)
    own = gather_plane(jnp.concatenate([w_in, w_out], axis=1), tables)
    blocks = gather_blocks(own, tables, members)
    rows, _ = lax.optimization_barrier((rows, own))
    rows = swap_digits(rows, tables, members)
    rows = deliver_unrolls(rows, tables, members)
    observed = rows[:, : steps + 1].transpose(1, 0, 2)
    used_rows = rows[:, steps + 1, 0].astype(f32)
    actions = lax.dynamic_index_in_dim(
        actions.reshape(steps, share, members), member, 2, keepdims=False
    )
    rewards = lax.dynamic_index_in_dim(
        rewards.reshape(steps, share, members), member, 2, keepdims=False
    )
    flat_obs = observed.reshape((steps + 1) * share, features).astype(f32)
    target_in = (flat_obs * inverse_scale(flat_obs) * gain).astype(bf16)
    target_logits = jnp.dot(target_in, w_pol, preferred_element_type=f32)
    target_values = jnp.dot(target_in, w_val, preferred_element_type=f32).reshape(
        steps + 1, share
    )
    policy_targets = jax.nn.softmax(target_logits, axis=-1)
    value_targets = jnp.concatenate(
        [rewards + discount * target_values[1:], target_values[steps:]], axis=0
    )
    action_ids = jnp.arange(num_actions, dtype=jnp.int32)
    onehots = (actions.reshape(-1)[:, None] == action_ids[None, :]).astype(bf16)
    emb = jnp.dot(onehots, embed, preferred_element_type=f32).astype(bf16)
    feature_ids = jnp.arange(features, dtype=jnp.int32)
    order = (feature_ids % (features // 2)) // 8 * 16 + feature_ids // (features // 2) * 8 + feature_ids % 8
    unorder = (order[:, None] == feature_ids[None, :]).astype(bf16)
    starts = lax.dot_general(
        jnp.concatenate([emb, observed[0]], axis=0),
        unorder,
        (((1,), (1,)), ((), ())),
        preferred_element_type=f32,
    ).astype(bf16)

    def ordered(values):
        by_rows = values.reshape(features // 16, 2, 8, *values.shape[1:])
        return jnp.swapaxes(by_rows, 0, 1).reshape(values.shape)

    row_weight = jnp.tile(used_rows / tables, steps + 1)
    mine, other = run_block(
        core.reshape(1),
        starts,
        actions,
        policy_targets,
        value_targets.reshape(-1, 1),
        row_weight[:, None],
        ordered(w_pol),
        ordered(w_val)[None, :],
        ordered(gain)[None, :],
        blocks,
        unorder,
        tables // 2,
    )
    rows = reduce_partials(mine, other, tables, members)
    out_pol = rows[:, :num_actions]
    out_val = rows[:, num_actions] + rows[:, num_actions + 1]
    out_embed = rows[:, num_actions + 128 :].reshape(num_actions // tables, features)
    return out_pol, out_embed, out_val


def solution(mesh):
    return jax.shard_map(
        per_device,
        mesh=mesh,
        in_specs=(
            P("table", None),
            P("table", None, None),
            P("table", None),
            P(None, "table"),
            P(None, "table"),
            P("table", "mp"),
            P("table", "mp"),
            P(),
            P(),
            P(),
            P(),
        ),
        out_specs=(P("table", None), P("table", None), P("table")),
        check_vma=False,
    )
```

```python
import functools
import jax
import jax.numpy as jnp
from jax import lax
from jax.experimental import pallas as pl
from jax.experimental.pallas import tpu as pltpu
from jax.sharding import PartitionSpec as P

discount = 0.997
epsilon = 1e-06
f32 = jnp.float32
bf16 = jnp.bfloat16


def dot_nn(a, b):
    return lax.dot_general(a, b, (((1,), (0,)), ((), ())), preferred_element_type=f32)


def dot_nt(a, b):
    return lax.dot_general(a, b, (((1,), (1,)), ((), ())), preferred_element_type=f32)


def inverse_scale(vector):
    return lax.rsqrt(jnp.mean(vector * vector, axis=-1, keepdims=True) + epsilon)


def norm_back(vector, upstream, gain):
    factor = inverse_scale(vector)
    unit_vec = vector * factor
    scaled = upstream * gain
    return factor * (scaled - unit_vec * jnp.mean(scaled * unit_vec, axis=-1, keepdims=True))


def block_kernel(
    steps, share, lines, halves,
    weights_hbm, unorder_hbm, core_ref, start_ref, keys_ref, targets_ref, value_targets_ref, weight_ref, w_pol_ref,
    w_val_ref, gain_ref, mine_ref, other_ref, weights, unorder, latents, mixeds, slopes, mixed_lows,
    lows, head_sums, sems,
):
    chips = mine_ref.shape[0]
    core = core_ref[0]
    width = lows.shape[1]
    parts = lows.shape[0] // (steps * share)
    depth, units = weights.shape[1], weights.shape[2] // 2
    spans = [slice(side * depth, (side + 1) * depth) for side in range(halves)]
    copies = [
        [
            pltpu.make_async_copy(
                weights_hbm.at[pl.ds((side * lines + line) * depth, depth), :],
                weights.at[side * lines + line],
                sems.at[side * lines + line],
            )
            for side in range(halves)
        ]
        for line in range(lines)
    ]
    for line_copies in copies:
        for copy in line_copies:
            copy.start()
    unorder_copy = pltpu.make_async_copy(unorder_hbm, unorder, sems.at[halves * lines])
    unorder_copy.start()
    gain = gain_ref[...]

    def rows_of(position):
        start = position * share
        return pl.ds(start if isinstance(start, int) else pl.multiple_of(start, share), share)

    def forward(position, latent, arriving=False):
        here = rows_of(position)
        mixed = latent + start_ref[here, :].astype(f32)
        mixeds[here, :] = mixed
        normed = (mixed * inverse_scale(mixed) * gain).astype(bf16)
        totals = [0.0] * halves
        hiddens = []

        def add_line(line):
            for side in range(halves):
                product = dot_nt(weights[side * lines + line, :, units:], hiddens[line])
                totals[side] = totals[side] + product

        for line in range(lines):
            if arriving:
                for copy in copies[line]:
                    copy.wait()
            preact = sum(
                dot_nn(normed[:, span], weights[side * lines + line, :, :units])
                for side, span in enumerate(spans)
            )
            sig = 1.0 / (1.0 + jnp.exp(-preact))
            slopes[here, line * units:(line + 1) * units] = sig * (1.0 + preact * (1.0 - sig))
            hiddens.append((preact * sig).astype(bf16))
            if line > 0:
                add_line(line - 1)
        for line in range(lines - 1, lines):
            add_line(line)
        total = jnp.concatenate(totals, axis=0).T
        latent = mixed + total
        latents[rows_of(position + 1), :] = latent
        return latent

    first = start_ref[steps * share:, :].astype(f32)
    latents[:share, :] = first
    lax.fori_loop(1, steps, forward, forward(0, first, arriving=True))

    stacked = latents[...]
    scale = inverse_scale(stacked)
    head_in = (stacked * scale * gain).astype(bf16)
    logits = dot_nn(head_in, w_pol_ref[...])
    w_val = w_val_ref[...].astype(f32)
    values = jnp.sum(head_in.astype(f32) * w_val, axis=-1, keepdims=True)
    weight = weight_ref[...]
    exped = jnp.exp(logits - jnp.max(logits, axis=-1, keepdims=True))
    probs = exped / jnp.sum(exped, axis=-1, keepdims=True)
    logit_grad = (weight * (probs - targets_ref[...])).astype(bf16)
    value_grad = 2.0 * weight * (values - value_targets_ref[...])
    high = value_grad.astype(bf16)
    low = (value_grad - high.astype(f32)).astype(bf16)
    lane = lax.broadcasted_iota(jnp.int32, (value_grad.shape[0], 128), 1)
    value_lanes = jnp.where(lane == 0, high, jnp.where(lane == 1, low, jnp.zeros_like(low)))
    head_grads = jnp.concatenate([logit_grad, value_lanes], axis=1)
    sums = lax.dot_general(
        head_in, head_grads, (((0,), (0,)), ((), ())), preferred_element_type=f32
    )
    head_sums[...] = sums.reshape(head_sums.shape)
    columns = sums.shape[1]
    mine_ref[:, :, :columns] = head_sums[core].astype(bf16)
    other_ref[:, :, :columns] = head_sums[1 - core].astype(bf16)
    head_grad = dot_nt(logit_grad, w_pol_ref[...]) + value_grad * w_val
    unit_vec = stacked * scale
    scaled = head_grad * gain
    latents[...] = scale * (scaled - unit_vec * jnp.mean(scaled * unit_vec, axis=-1, keepdims=True))

    def backward(index, cotangent):
        position = steps - 1 - index
        here = rows_of(position)
        low = cotangent.astype(bf16)
        preact_grads = []
        for line in range(lines):
            hidden_grad = sum(
                dot_nn(low[:, span], weights[side * lines + line, :, units:])
                for side, span in enumerate(spans)
            )
            slope = slopes[here, line * units:(line + 1) * units]
            preact_grads.append((hidden_grad * slope).astype(bf16))
        total = jnp.concatenate(
            [
                sum(
                    dot_nt(weights[side * lines + line, :, :units], preact_grads[line])
                    for line in range(lines)
                )
                for side in range(halves)
            ],
            axis=0,
        ).T
        mixed_grad = cotangent + norm_back(mixeds[here, :], total, gain)
        mixed_lows[here, :] = mixed_grad.astype(bf16)
        return mixed_grad + latents[here, :]

    lax.fori_loop(0, steps, backward, latents[steps * share:, :])

    unorder_copy.wait()
    for quarter in range(parts):
        quarter_lows = dot_nn(mixed_lows[...], unorder[:, quarter * width:(quarter + 1) * width])
        lows[quarter * steps * share:(quarter + 1) * steps * share, :] = quarter_lows.astype(bf16)
    row = lax.broadcasted_iota(jnp.int32, (chips * 8, keys_ref.shape[1]), 0)
    row_key = 2 * row - (row & 7)
    for side, target in ((core, mine_ref), (1 - core, other_ref)):
        picks = jnp.where(row_key + 8 * side == keys_ref[...], 1.0, 0.0).astype(bf16)
        summed = dot_nn(picks, lows[...]).reshape(chips, 8, width)
        target[:, :, columns:] = summed.astype(target.dtype)


def run_block(
    core, starts, actions, targets, value_targets, weight, w_pol, w_val, gain, blocks, unorder, chips
):
    steps, share = actions.shape
    features = starts.shape[1]
    halves = 2
    depth = features // halves
    units = blocks.shape[1] // 2
    lines = blocks.shape[0] // features
    rows = (steps + 1) * share
    num_actions = w_pol.shape[1]
    parts = 8 * chips * 2 // num_actions
    width = features // parts
    columns = num_actions + 128 + width
    quarters = jnp.arange(parts, dtype=jnp.int32)
    keys = (actions.reshape(1, -1) * parts + quarters[:, None]).reshape(1, -1)
    vmem = pl.BlockSpec(memory_space=pltpu.VMEM)
    return pl.pallas_call(
        functools.partial(block_kernel, steps, share, lines, halves),
        out_shape=(
            jax.ShapeDtypeStruct((chips, 8, columns), bf16),
            jax.ShapeDtypeStruct((chips, 8, columns), bf16),
        ),
        in_specs=[pl.BlockSpec(memory_space=pltpu.HBM)] * 2
        + [pl.BlockSpec(memory_space=pltpu.SMEM)]
        + [vmem] * 8,
        out_specs=(vmem,) * 2,
        scratch_shapes=[
            pltpu.VMEM((halves * lines, depth, 2 * units), bf16),
            pltpu.VMEM((features, features), bf16),
            pltpu.VMEM((rows, features), f32),
            pltpu.VMEM((steps * share, features), f32),
            pltpu.VMEM((steps * share, lines * units), f32),
            pltpu.VMEM((steps * share, features), bf16),
            pltpu.VMEM((parts * steps * share, width), bf16),
            pltpu.VMEM((halves, chips, 8, num_actions + 128), f32),
            pltpu.SemaphoreType.DMA((halves * lines + 1,)),
        ],
        compiler_params=pltpu.CompilerParams(vmem_limit_bytes=57 * 1024 * 1024),
        cost_estimate=pl.CostEstimate(flops=3 * 10**9, bytes_accessed=10**7, transcendentals=0),
    )(blocks, unorder, core, starts, keys, targets, value_targets, weight, w_pol, w_val, gain)


def cores_swap(value, tables):
    return lax.ppermute(value, "table", [(t, t ^ 1) for t in range(tables)])


def along_x(value, step, members):
    return lax.ppermute(value, "mp", [(m, (m + step) % members) for m in range(members)])


def same_core_groups(tables):
    return [[2 * k + c for k in range(tables // 2)] for c in range(2)]


def gather_plane(rows, tables):
    return lax.all_to_all(
        jnp.tile(rows, (tables // 2, 1)),
        "table",
        split_axis=0,
        concat_axis=0,
        tiled=True,
        axis_index_groups=same_core_groups(tables),
    )


def gather_blocks(own, tables, members):
    groups = [
        [(2 * k + c) * members + m for c in range(2) for m in range(members)]
        for k in range(tables // 2)
    ]
    return lax.all_gather(own, ("table", "mp"), axis=0, tiled=True, axis_index_groups=groups)


def pick_unrolls(replay, request_rows, request_count, steps, member, tables, members):
    share = tables // members
    width = replay.shape[1]
    firsts = request_rows[0, :, 0].reshape(share, members)
    firsts = lax.dynamic_index_in_dim(firsts, member, 1, keepdims=False)
    counts = lax.dynamic_index_in_dim(
        request_count[0].reshape(share, members), member, 1, keepdims=False
    )
    used = (counts > 0).astype(f32)
    offsets = jnp.arange(8, dtype=jnp.int32)
    positions = firsts[:, None] + offsets[None, :]
    row_ids = jnp.arange(replay.shape[0], dtype=jnp.int32)
    picks = (positions.reshape(-1)[:, None] == row_ids[None, :]).astype(bf16)
    rows = jnp.dot(picks, replay, preferred_element_type=f32).reshape(share, 8, width)
    rows = jnp.where(offsets[None, :, None] <= steps, rows, used[:, None, None])
    return rows.astype(bf16)


def swap_digits(rows, tables, members):
    share = tables // members
    swap = [
        ((members * a + b) * members + d, (members * a + d) * members + b)
        for a in range(share)
        for b in range(members)
        for d in range(members)
    ]
    return lax.ppermute(rows, ("table", "mp"), swap)


def deliver_unrolls(rows, tables, members):
    share = tables // members
    groups = [[members * a + d for a in range(share)] for d in range(members)]
    return lax.all_to_all(
        rows, "table", split_axis=0, concat_axis=0, tiled=True, axis_index_groups=groups
    )


def reduce_partials(mine, other, tables, members):
    got = cores_swap(other, tables)
    summed = (mine.astype(f32) + got.astype(f32)).astype(bf16)
    parts = lax.all_to_all(
        summed,
        "table",
        split_axis=0,
        concat_axis=0,
        tiled=True,
        axis_index_groups=same_core_groups(tables),
    )
    summed = jnp.sum(parts.astype(f32), axis=0)
    copies = jnp.broadcast_to(summed[None], (members, *summed.shape))
    return lax.all_to_all(copies, "mp", split_axis=0, concat_axis=0, tiled=True)


def unpack_kernel(terms_ref, pol_ref, embed_ref, val_ref):
    rows = jnp.sum(terms_ref[...], axis=0)
    num_actions = pol_ref.shape[1]
    pol_ref[...] = rows[:, :num_actions]
    value = rows[:, num_actions:num_actions + 1] + rows[:, num_actions + 1:num_actions + 2]
    val_ref[...] = jnp.broadcast_to(value, (rows.shape[0], 128)).T[:1, :]
    actions = embed_ref.shape[0]
    parts = rows.shape[0] // actions
    start = num_actions + 128
    width = rows.shape[1] - start
    for action in range(actions):
        for part in range(parts):
            row = action * parts + part
            embed_ref[action:action + 1, part * width:(part + 1) * width] = rows[row:row + 1, start:]


def unpack_gradients(terms, num_actions, actions):
    rows, columns = terms.shape[1:]
    parts = rows // actions
    pol, embed, val = pl.pallas_call(
        unpack_kernel,
        out_shape=(
            jax.ShapeDtypeStruct((rows, num_actions), f32),
            jax.ShapeDtypeStruct((actions, parts * (columns - num_actions - 128)), f32),
            jax.ShapeDtypeStruct((1, rows), f32),
        ),
        in_specs=[pl.BlockSpec(memory_space=pltpu.VMEM)],
        out_specs=(pl.BlockSpec(memory_space=pltpu.VMEM),) * 3,
    )(terms)
    return pol, embed, val.reshape(rows)


def per_device(
    replay, request_rows, request_count, actions, rewards, w_in, w_out, w_pol, w_val, embed, gain
):
    tables = lax.axis_size("table")
    members = lax.axis_size("mp")
    member = lax.axis_index("mp")
    core = lax.axis_index("table") % 2
    share = tables // members
    features = replay.shape[1]
    steps = actions.shape[0]
    num_actions = w_pol.shape[1]
    rows = pick_unrolls(replay, request_rows, request_count, steps, member, tables, members)
    own = gather_plane(jnp.concatenate([w_in, w_out], axis=1), tables)
    blocks = gather_blocks(own, tables, members)
    rows, _ = lax.optimization_barrier((rows, own))
    rows = swap_digits(rows, tables, members)
    rows = deliver_unrolls(rows, tables, members)
    observed = rows[:, : steps + 1].transpose(1, 0, 2)
    used_rows = rows[:, steps + 1, 0].astype(f32)
    actions = lax.dynamic_index_in_dim(
        actions.reshape(steps, share, members), member, 2, keepdims=False
    )
    rewards = lax.dynamic_index_in_dim(
        rewards.reshape(steps, share, members), member, 2, keepdims=False
    )
    flat_obs = observed.reshape((steps + 1) * share, features).astype(f32)
    target_in = (flat_obs * inverse_scale(flat_obs) * gain).astype(bf16)
    target_logits = jnp.dot(target_in, w_pol, preferred_element_type=f32)
    target_values = jnp.dot(target_in, w_val, preferred_element_type=f32).reshape(
        steps + 1, share
    )
    policy_targets = jax.nn.softmax(target_logits, axis=-1)
    value_targets = jnp.concatenate(
        [rewards + discount * target_values[1:], target_values[steps:]], axis=0
    )
    action_ids = jnp.arange(num_actions, dtype=jnp.int32)
    onehots = (actions.reshape(-1)[:, None] == action_ids[None, :]).astype(bf16)
    emb = jnp.dot(onehots, embed, preferred_element_type=f32).astype(bf16)
    feature_ids = jnp.arange(features, dtype=jnp.int32)
    order = (feature_ids % (features // 2)) // 8 * 16 + feature_ids // (features // 2) * 8 + feature_ids % 8
    unorder = (order[:, None] == feature_ids[None, :]).astype(bf16)
    starts = lax.dot_general(
        jnp.concatenate([emb, observed[0]], axis=0),
        unorder,
        (((1,), (1,)), ((), ())),
        preferred_element_type=f32,
    ).astype(bf16)

    def ordered(values):
        by_rows = values.reshape(features // 16, 2, 8, *values.shape[1:])
        return jnp.swapaxes(by_rows, 0, 1).reshape(values.shape)

    row_weight = jnp.tile(used_rows / tables, steps + 1)
    mine, other = run_block(
        core.reshape(1),
        starts,
        actions,
        policy_targets,
        value_targets.reshape(-1, 1),
        row_weight[:, None],
        ordered(w_pol),
        ordered(w_val)[None, :],
        ordered(gain)[None, :],
        blocks,
        unorder,
        tables // 2,
    )
    terms = reduce_partials(mine, other, tables, members)
    return unpack_gradients(terms, num_actions, num_actions // tables)


def solution(mesh):
    return jax.shard_map(
        per_device,
        mesh=mesh,
        in_specs=(
            P("table", None),
            P("table", None, None),
            P("table", None),
            P(None, "table"),
            P(None, "table"),
            P("table", "mp"),
            P("table", "mp"),
            P(),
            P(),
            P(),
            P(),
        ),
        out_specs=(P("table", None), P("table", None), P("table")),
        check_vma=False,
    )
```

```python
import functools
import jax
import jax.numpy as jnp
from jax import lax
from jax.experimental import pallas as pl
from jax.experimental.pallas import tpu as pltpu
from jax.sharding import PartitionSpec as P

discount = 0.997
epsilon = 1e-06
f32 = jnp.float32
bf16 = jnp.bfloat16


def dot_nn(a, b):
    return lax.dot_general(a, b, (((1,), (0,)), ((), ())), preferred_element_type=f32)


def dot_nt(a, b):
    return lax.dot_general(a, b, (((1,), (1,)), ((), ())), preferred_element_type=f32)


def dot_nt_rows(a, b):
    rows = a.shape[0] // 2
    return jnp.concatenate([dot_nt(a[:rows], b), dot_nt(a[rows:], b)], axis=0)


def inverse_scale(vector):
    return lax.rsqrt(jnp.mean(vector * vector, axis=-1, keepdims=True) + epsilon)


def norm_back(vector, upstream, gain):
    factor = inverse_scale(vector)
    unit_vec = vector * factor
    scaled = upstream * gain
    return factor * (scaled - unit_vec * jnp.mean(scaled * unit_vec, axis=-1, keepdims=True))


def block_kernel(
    steps, share, lines, halves,
    weights_hbm, unorder_hbm, core_ref, start_ref, keys_ref, targets_ref, value_targets_ref, weight_ref, w_pol_ref,
    w_val_ref, gain_ref, mine_ref, other_ref, weights, unorder, latents, mixeds, slopes, mixed_lows,
    lows, head_sums, sems,
):
    chips = mine_ref.shape[0]
    core = core_ref[0]
    width = lows.shape[1]
    parts = lows.shape[0] // (steps * share)
    depth, units = weights.shape[1], weights.shape[2] // 2
    spans = [slice(side * depth, (side + 1) * depth) for side in range(halves)]
    copies = [
        [
            pltpu.make_async_copy(
                weights_hbm.at[pl.ds((side * lines + line) * depth, depth), :],
                weights.at[side * lines + line],
                sems.at[side * lines + line],
            )
            for side in range(halves)
        ]
        for line in range(lines)
    ]
    for line_copies in copies:
        for copy in line_copies:
            copy.start()
    unorder_copy = pltpu.make_async_copy(unorder_hbm, unorder, sems.at[halves * lines])
    unorder_copy.start()
    gain = gain_ref[...]

    def rows_of(position):
        start = position * share
        return pl.ds(start if isinstance(start, int) else pl.multiple_of(start, share), share)

    def forward(position, latent, arriving=False):
        here = rows_of(position)
        mixed = latent + start_ref[here, :].astype(f32)
        mixeds[here, :] = mixed
        normed = (mixed * inverse_scale(mixed) * gain).astype(bf16)
        totals = [0.0] * halves
        hiddens = []

        def add_line(line):
            for side in range(halves):
                product = dot_nt_rows(weights[side * lines + line, :, units:], hiddens[line])
                totals[side] = totals[side] + product

        for line in range(lines):
            if arriving:
                for copy in copies[line]:
                    copy.wait()
            preact = sum(
                dot_nn(normed[:, span], weights[side * lines + line, :, :units])
                for side, span in enumerate(spans)
            )
            sig = 1.0 / (1.0 + jnp.exp(-preact))
            slopes[here, line * units:(line + 1) * units] = sig * (1.0 + preact * (1.0 - sig))
            hiddens.append((preact * sig).astype(bf16))
            if line > 0:
                add_line(line - 1)
        for line in range(lines - 1, lines):
            add_line(line)
        total = jnp.concatenate(totals, axis=0).T
        latent = mixed + total
        latents[rows_of(position + 1), :] = latent
        return latent

    first = start_ref[steps * share:, :].astype(f32)
    latents[:share, :] = first
    lax.fori_loop(1, steps, forward, forward(0, first, arriving=True))

    stacked = latents[...]
    scale = inverse_scale(stacked)
    head_in = (stacked * scale * gain).astype(bf16)
    logits = dot_nn(head_in, w_pol_ref[...])
    w_val = w_val_ref[...].astype(f32)
    values = jnp.sum(head_in.astype(f32) * w_val, axis=-1, keepdims=True)
    weight = weight_ref[...]
    exped = jnp.exp(logits - jnp.max(logits, axis=-1, keepdims=True))
    probs = exped / jnp.sum(exped, axis=-1, keepdims=True)
    logit_grad = (weight * (probs - targets_ref[...])).astype(bf16)
    value_grad = 2.0 * weight * (values - value_targets_ref[...])
    high = value_grad.astype(bf16)
    low = (value_grad - high.astype(f32)).astype(bf16)
    lane = lax.broadcasted_iota(jnp.int32, (value_grad.shape[0], 128), 1)
    value_lanes = jnp.where(lane == 0, high, jnp.where(lane == 1, low, jnp.zeros_like(low)))
    head_grads = jnp.concatenate([logit_grad, value_lanes], axis=1)
    sums = lax.dot_general(
        head_in, head_grads, (((0,), (0,)), ((), ())), preferred_element_type=f32
    )
    head_sums[...] = sums.reshape(head_sums.shape)
    columns = sums.shape[1]
    mine_ref[:, :, :columns] = head_sums[core].astype(bf16)
    other_ref[:, :, :columns] = head_sums[1 - core].astype(bf16)
    head_grad = dot_nt(logit_grad, w_pol_ref[...]) + value_grad * w_val
    unit_vec = stacked * scale
    scaled = head_grad * gain
    latents[...] = scale * (scaled - unit_vec * jnp.mean(scaled * unit_vec, axis=-1, keepdims=True))

    def backward(index, cotangent):
        position = steps - 1 - index
        here = rows_of(position)
        low = cotangent.astype(bf16)
        preact_grads = []
        for line in range(lines):
            hidden_grad = sum(
                dot_nn(low[:, span], weights[side * lines + line, :, units:])
                for side, span in enumerate(spans)
            )
            slope = slopes[here, line * units:(line + 1) * units]
            preact_grads.append((hidden_grad * slope).astype(bf16))
        total = jnp.concatenate(
            [
                sum(
                    dot_nt_rows(weights[side * lines + line, :, :units], preact_grads[line])
                    for line in range(lines)
                )
                for side in range(halves)
            ],
            axis=0,
        ).T
        mixed_grad = cotangent + norm_back(mixeds[here, :], total, gain)
        mixed_lows[here, :] = mixed_grad.astype(bf16)
        return mixed_grad + latents[here, :]

    lax.fori_loop(0, steps, backward, latents[steps * share:, :])

    unorder_copy.wait()
    for quarter in range(parts):
        quarter_lows = dot_nn(mixed_lows[...], unorder[:, quarter * width:(quarter + 1) * width])
        lows[quarter * steps * share:(quarter + 1) * steps * share, :] = quarter_lows.astype(bf16)
    row = lax.broadcasted_iota(jnp.int32, (chips * 8, keys_ref.shape[1]), 0)
    row_key = 2 * row - (row & 7)
    for side, target in ((core, mine_ref), (1 - core, other_ref)):
        picks = jnp.where(row_key + 8 * side == keys_ref[...], 1.0, 0.0).astype(bf16)
        summed = dot_nn(picks, lows[...]).reshape(chips, 8, width)
        target[:, :, columns:] = summed.astype(target.dtype)


def run_block(
    core, starts, actions, targets, value_targets, weight, w_pol, w_val, gain, blocks, unorder, chips
):
    steps, share = actions.shape
    features = starts.shape[1]
    halves = 2
    depth = features // halves
    units = blocks.shape[1] // 2
    lines = blocks.shape[0] // features
    rows = (steps + 1) * share
    num_actions = w_pol.shape[1]
    parts = 8 * chips * 2 // num_actions
    width = features // parts
    columns = num_actions + 128 + width
    quarters = jnp.arange(parts, dtype=jnp.int32)
    keys = (actions.reshape(1, -1) * parts + quarters[:, None]).reshape(1, -1)
    vmem = pl.BlockSpec(memory_space=pltpu.VMEM)
    return pl.pallas_call(
        functools.partial(block_kernel, steps, share, lines, halves),
        out_shape=(
            jax.ShapeDtypeStruct((chips, 8, columns), bf16),
            jax.ShapeDtypeStruct((chips, 8, columns), bf16),
        ),
        in_specs=[pl.BlockSpec(memory_space=pltpu.HBM)] * 2
        + [pl.BlockSpec(memory_space=pltpu.SMEM)]
        + [vmem] * 8,
        out_specs=(vmem,) * 2,
        scratch_shapes=[
            pltpu.VMEM((halves * lines, depth, 2 * units), bf16),
            pltpu.VMEM((features, features), bf16),
            pltpu.VMEM((rows, features), f32),
            pltpu.VMEM((steps * share, features), f32),
            pltpu.VMEM((steps * share, lines * units), f32),
            pltpu.VMEM((steps * share, features), bf16),
            pltpu.VMEM((parts * steps * share, width), bf16),
            pltpu.VMEM((halves, chips, 8, num_actions + 128), f32),
            pltpu.SemaphoreType.DMA((halves * lines + 1,)),
        ],
        compiler_params=pltpu.CompilerParams(vmem_limit_bytes=57 * 1024 * 1024),
        cost_estimate=pl.CostEstimate(flops=3 * 10**9, bytes_accessed=10**7, transcendentals=0),
    )(blocks, unorder, core, starts, keys, targets, value_targets, weight, w_pol, w_val, gain)


def cores_swap(value, tables):
    return lax.ppermute(value, "table", [(t, t ^ 1) for t in range(tables)])


def along_x(value, step, members):
    return lax.ppermute(value, "mp", [(m, (m + step) % members) for m in range(members)])


def same_core_groups(tables):
    return [[2 * k + c for k in range(tables // 2)] for c in range(2)]


def gather_plane(rows, tables):
    return lax.all_to_all(
        jnp.tile(rows, (tables // 2, 1)),
        "table",
        split_axis=0,
        concat_axis=0,
        tiled=True,
        axis_index_groups=same_core_groups(tables),
    )


def gather_blocks(own, tables, members):
    groups = [
        [(2 * k + c) * members + m for c in range(2) for m in range(members)]
        for k in range(tables // 2)
    ]
    return lax.all_gather(own, ("table", "mp"), axis=0, tiled=True, axis_index_groups=groups)


def pick_unrolls(replay, request_rows, request_count, steps, member, tables, members):
    share = tables // members
    width = replay.shape[1]
    firsts = request_rows[0, :, 0].reshape(share, members)
    firsts = lax.dynamic_index_in_dim(firsts, member, 1, keepdims=False)
    counts = lax.dynamic_index_in_dim(
        request_count[0].reshape(share, members), member, 1, keepdims=False
    )
    used = (counts > 0).astype(f32)
    offsets = jnp.arange(8, dtype=jnp.int32)
    positions = firsts[:, None] + offsets[None, :]
    row_ids = jnp.arange(replay.shape[0], dtype=jnp.int32)
    picks = (positions.reshape(-1)[:, None] == row_ids[None, :]).astype(bf16)
    rows = jnp.dot(picks, replay, preferred_element_type=f32).reshape(share, 8, width)
    rows = jnp.where(offsets[None, :, None] <= steps, rows, used[:, None, None])
    return rows.astype(bf16)


def swap_digits(rows, tables, members):
    share = tables // members
    swap = [
        ((members * a + b) * members + d, (members * a + d) * members + b)
        for a in range(share)
        for b in range(members)
        for d in range(members)
    ]
    return lax.ppermute(rows, ("table", "mp"), swap)


def deliver_unrolls(rows, tables, members):
    share = tables // members
    groups = [[members * a + d for a in range(share)] for d in range(members)]
    return lax.all_to_all(
        rows, "table", split_axis=0, concat_axis=0, tiled=True, axis_index_groups=groups
    )


def reduce_partials(mine, other, tables, members):
    got = cores_swap(other, tables)
    summed = (mine.astype(f32) + got.astype(f32)).astype(bf16)
    parts = lax.all_to_all(
        summed,
        "table",
        split_axis=0,
        concat_axis=0,
        tiled=True,
        axis_index_groups=same_core_groups(tables),
    )
    summed = jnp.sum(parts.astype(f32), axis=0)
    copies = jnp.broadcast_to(summed[None], (members, *summed.shape))
    return lax.all_to_all(copies, "mp", split_axis=0, concat_axis=0, tiled=True)


def unpack_kernel(terms_ref, pol_ref, embed_ref, val_ref):
    rows = jnp.sum(terms_ref[...], axis=0)
    num_actions = pol_ref.shape[1]
    pol_ref[...] = rows[:, :num_actions]
    value = rows[:, num_actions:num_actions + 1] + rows[:, num_actions + 1:num_actions + 2]
    val_ref[...] = jnp.broadcast_to(value, (rows.shape[0], 128)).T[:1, :]
    actions = embed_ref.shape[0]
    parts = rows.shape[0] // actions
    start = num_actions + 128
    width = rows.shape[1] - start
    for action in range(actions):
        for part in range(parts):
            row = action * parts + part
            embed_ref[action:action + 1, part * width:(part + 1) * width] = rows[row:row + 1, start:]


def unpack_gradients(terms, num_actions, actions):
    rows, columns = terms.shape[1:]
    parts = rows // actions
    pol, embed, val = pl.pallas_call(
        unpack_kernel,
        out_shape=(
            jax.ShapeDtypeStruct((rows, num_actions), f32),
            jax.ShapeDtypeStruct((actions, parts * (columns - num_actions - 128)), f32),
            jax.ShapeDtypeStruct((1, rows), f32),
        ),
        in_specs=[pl.BlockSpec(memory_space=pltpu.VMEM)],
        out_specs=(pl.BlockSpec(memory_space=pltpu.VMEM),) * 3,
    )(terms)
    return pol, embed, val.reshape(rows)


def per_device(
    replay, request_rows, request_count, actions, rewards, w_in, w_out, w_pol, w_val, embed, gain
):
    tables = lax.axis_size("table")
    members = lax.axis_size("mp")
    member = lax.axis_index("mp")
    core = lax.axis_index("table") % 2
    share = tables // members
    features = replay.shape[1]
    steps = actions.shape[0]
    num_actions = w_pol.shape[1]
    rows = pick_unrolls(replay, request_rows, request_count, steps, member, tables, members)
    own = gather_plane(jnp.concatenate([w_in, w_out], axis=1), tables)
    blocks = gather_blocks(own, tables, members)
    rows, _ = lax.optimization_barrier((rows, own))
    rows = swap_digits(rows, tables, members)
    rows = deliver_unrolls(rows, tables, members)
    observed = rows[:, : steps + 1].transpose(1, 0, 2)
    used_rows = rows[:, steps + 1, 0].astype(f32)
    actions = lax.dynamic_index_in_dim(
        actions.reshape(steps, share, members), member, 2, keepdims=False
    )
    rewards = lax.dynamic_index_in_dim(
        rewards.reshape(steps, share, members), member, 2, keepdims=False
    )
    flat_obs = observed.reshape((steps + 1) * share, features).astype(f32)
    target_in = (flat_obs * inverse_scale(flat_obs) * gain).astype(bf16)
    target_logits = jnp.dot(target_in, w_pol, preferred_element_type=f32)
    target_values = jnp.dot(target_in, w_val, preferred_element_type=f32).reshape(
        steps + 1, share
    )
    policy_targets = jax.nn.softmax(target_logits, axis=-1)
    value_targets = jnp.concatenate(
        [rewards + discount * target_values[1:], target_values[steps:]], axis=0
    )
    action_ids = jnp.arange(num_actions, dtype=jnp.int32)
    onehots = (actions.reshape(-1)[:, None] == action_ids[None, :]).astype(bf16)
    emb = jnp.dot(onehots, embed, preferred_element_type=f32).astype(bf16)
    feature_ids = jnp.arange(features, dtype=jnp.int32)
    order = (feature_ids % (features // 2)) // 8 * 16 + feature_ids // (features // 2) * 8 + feature_ids % 8
    unorder = (order[:, None] == feature_ids[None, :]).astype(bf16)
    starts = lax.dot_general(
        jnp.concatenate([emb, observed[0]], axis=0),
        unorder,
        (((1,), (1,)), ((), ())),
        preferred_element_type=f32,
    ).astype(bf16)

    def ordered(values):
        by_rows = values.reshape(features // 16, 2, 8, *values.shape[1:])
        return jnp.swapaxes(by_rows, 0, 1).reshape(values.shape)

    row_weight = jnp.tile(used_rows / tables, steps + 1)
    mine, other = run_block(
        core.reshape(1),
        starts,
        actions,
        policy_targets,
        value_targets.reshape(-1, 1),
        row_weight[:, None],
        ordered(w_pol),
        ordered(w_val)[None, :],
        ordered(gain)[None, :],
        blocks,
        unorder,
        tables // 2,
    )
    terms = reduce_partials(mine, other, tables, members)
    return unpack_gradients(terms, num_actions, num_actions // tables)


def solution(mesh):
    return jax.shard_map(
        per_device,
        mesh=mesh,
        in_specs=(
            P("table", None),
            P("table", None, None),
            P("table", None),
            P(None, "table"),
            P(None, "table"),
            P("table", "mp"),
            P("table", "mp"),
            P(),
            P(),
            P(),
            P(),
        ),
        out_specs=(P("table", None), P("table", None), P("table")),
        check_vma=False,
    )
```
